32 devices in a mesh: ctx: 8 (over z, x), ch: 4 (over y, core).
Axes of the slice: x: 2, y: 2, z: 4, core: 2. Of those that a mesh axis runs over, the one named last changes fastest.
Arguments:
- query_act: bfloat16 [1024, 4096], P('ctx', 'ch'), may hold values from -6 to 6
- key_act: bfloat16 [1024, 4096], P('ctx', 'ch'), may hold values from -6 to 6
- value_act: bfloat16 [1024, 4096], P('ctx', 'ch'), may hold values from -6 to 6
- filters: bfloat16 [256, 128], P('ch'), may hold values from -0.5 to 0.5
- skip_bias: float32 [4096], P('ch'), may hold values from -4 to 4
- out_weight: bfloat16 [4096, 8192], P('ch'), may hold values from -0.09375 to 0.09375
- out_grad: bfloat16 [1024, 8192], P('ctx', 'ch'), may hold values from -6 to 6
Outputs:
- gated: bfloat16 [1024, 4096], P('ctx', 'ch')
- query_grad: bfloat16 [1024, 4096], P('ctx', 'ch')
- key_grad: bfloat16 [1024, 4096], P('ctx', 'ch')
- value_grad: bfloat16 [1024, 4096], P('ctx', 'ch')
- filter_grad: float32 [256, 128], P('ch')
- skip_grad: float32 [4096], P('ch')
The draws below stay inside these ranges and needn't reach their ends.
All inputs are finite; a program needn't handle non-finite values.
Results may differ from the reference program's by a relative error of at most 0.0075.
Values may be sent and summed in bfloat16 or wider, within the bound.
A program may use at most 64 MiB of HBM per device.

```python
import jax
import jax.numpy as jnp
from jax import lax

C = 4096
DOUT = 8192
GSIZE = 16
TAPS = 128
TOKENS = 1024
GROUPS = 256


def level_of(own_key, shape, shards, low, top_value):
    level = 1.0
    for position, parts in shards:
        steps = jax.random.uniform(jax.random.fold_in(jax.random.fold_in(own_key, 6), position), (parts,), jnp.float32, low / len(shards), top_value / len(shards))
        level = level * jnp.repeat(jnp.exp(steps), shape[position] // parts).reshape((-1,) + (1,) * (len(shape) - 1 - position))
    return level


def bell_draw(rng, shape, spread, bound, split=(), kind=jnp.bfloat16):
    drawn = jax.random.normal(rng, shape, jnp.float32) * spread
    if len(split) > 0:
        drawn = level_of(rng, shape, split, -0.22, 0.18) * drawn
    return jnp.clip(drawn, min=-bound, max=bound).astype(kind)


def setup_inputs(seed: int = 0) -> dict:
    splits = jax.random.split(jax.random.key(seed), 8)
    query_act = bell_draw(splits[0], (TOKENS, C), 1.0, 6.0, ((0, 8), (1, 4)))
    key_act = bell_draw(splits[1], (TOKENS, C), 1.0, 6.0, ((0, 8), (1, 4)))
    value_act = bell_draw(splits[2], (TOKENS, C), 1.0, 6.0, ((0, 8), (1, 4)))
    filters = bell_draw(splits[3], (GROUPS, TAPS), TAPS ** -0.5, 0.5, ((0, 4),))
    skip_bias = bell_draw(splits[4], (C,), 1.0, 4.0, ((0, 4),), jnp.float32)
    out_weight = bell_draw(splits[5], (C, DOUT), C ** -0.5, 0.09375, ((0, 4),))
    out_grad = bell_draw(splits[6], (TOKENS, DOUT), 1.0, 6.0, ((0, 8), (1, 4)))
    return dict(query_act=query_act, key_act=key_act, value_act=value_act, filters=filters, skip_bias=skip_bias, out_weight=out_weight, out_grad=out_grad)


def filter_table(filt_blk, lag):
    valid = (lag >= 0) & (lag < TAPS)
    index_tab = jnp.clip(lag, 0, TAPS - 1)
    return jnp.where(valid[None], filt_blk[:, index_tab], jnp.zeros((), jnp.float32))


def reference(query_act, key_act, value_act, filters, skip_bias, out_weight, out_grad):
    blk = 256 if C % 256 == 0 else C
    nblk = C // blk
    gblk = blk // GSIZE
    nbt = TOKENS // TAPS
    rows_t = jnp.arange(TAPS, dtype=jnp.int32)[:, None]
    cols_s = jnp.arange(2 * TAPS - 1, dtype=jnp.int32)[None, :]
    fwd_lag = rows_t + (TAPS - 1) - cols_s
    bwd_lag = cols_s - rows_t
    taps_j = jnp.arange(TAPS, dtype=jnp.int32)[None, :]
    pick_idx = rows_t + (TAPS - 1) - taps_j

    def window_prev(series):
        blocks = series.reshape(nbt, TAPS, gblk, GSIZE)
        before = jnp.concatenate([jnp.zeros((1, TAPS, gblk, GSIZE), jnp.float32), blocks[:-1]], axis=0)
        return jnp.concatenate([before[:, 1:], blocks], axis=1)

    def window_next(series):
        blocks = series.reshape(nbt, TAPS, gblk, GSIZE)
        after = jnp.concatenate([blocks[1:], jnp.zeros((1, TAPS, gblk, GSIZE), jnp.float32)], axis=0)
        return jnp.concatenate([blocks, after[:, :TAPS - 1]], axis=1)

    def one_block(index):
        start = (index * blk).astype(jnp.int32)
        gstart = (index * gblk).astype(jnp.int32)
        query_f = lax.dynamic_slice_in_dim(query_act, start, blk, 1).astype(jnp.float32)
        key_f = lax.dynamic_slice_in_dim(key_act, start, blk, 1).astype(jnp.float32)
        value_f = lax.dynamic_slice_in_dim(value_act, start, blk, 1).astype(jnp.float32)
        filt = lax.dynamic_slice_in_dim(filters, gstart, gblk, 0).astype(jnp.float32)
        skip = lax.dynamic_slice_in_dim(skip_bias, start, blk, 0)
        weight_blk = lax.dynamic_slice_in_dim(out_weight, start, blk, 0)
        inner_f = (key_f * value_f).astype(jnp.bfloat16).astype(jnp.float32)
        inner_win = window_prev(inner_f)
        conv = jnp.einsum("gts,bsgc->btgc", filter_table(filt, fwd_lag), inner_win, precision=lax.Precision.HIGHEST).reshape(TOKENS, blk)
        mixed = conv + skip[None, :] * inner_f
        gated = (query_f * mixed).astype(jnp.bfloat16)
        mixed_grad = jnp.dot(out_grad, weight_blk.T, preferred_element_type=jnp.float32)
        query_grad = (mixed_grad * mixed).astype(jnp.bfloat16)
        conv_f = (mixed_grad * query_f).astype(jnp.bfloat16).astype(jnp.float32)
        grad_win = window_next(conv_f)
        back = jnp.einsum("gts,bsgc->btgc", filter_table(filt, bwd_lag), grad_win, precision=lax.Precision.HIGHEST).reshape(TOKENS, blk)
        inner_grad = back + skip[None, :] * conv_f
        key_grad = (inner_grad * value_f).astype(jnp.bfloat16)
        value_grad = (inner_grad * key_f).astype(jnp.bfloat16)
        pairs = jnp.einsum("btgc,bsgc->gts", conv_f.reshape(nbt, TAPS, gblk, GSIZE), inner_win, precision=lax.Precision.HIGHEST)
        picked = jnp.take_along_axis(pairs, jnp.broadcast_to(pick_idx[None], (gblk, TAPS, TAPS)), axis=2)
        filt_grad = jnp.sum(picked, axis=1)
        skip_grad = jnp.sum(conv_f * inner_f, axis=0)
        return gated, query_grad, key_grad, value_grad, filt_grad, skip_grad

    outs = lax.map(one_block, jnp.arange(nblk, dtype=jnp.int32))

    def joined(stack):
        return jnp.transpose(stack, (1, 0, 2)).reshape(TOKENS, C)

    return joined(outs[0]), joined(outs[1]), joined(outs[2]), joined(outs[3]), outs[4].reshape(GROUPS, TAPS), outs[5].reshape(C)
```

```python
import functools

import jax
import jax.numpy as jnp
from jax import lax
from jax.experimental import pallas as pl
from jax.experimental.pallas import tpu as pltpu
from jax.sharding import PartitionSpec as P

LANES = 128
PIECE = 256
MESH = pl.DeviceIdType.MESH
F32 = jnp.float32
BF16 = jnp.bfloat16
NT = (((1,), (1,)), ((), ()))


def kernel_body(n_ctx, n_ch, reduce_here, *refs):
    (q_ref, k_ref, v_ref, f_ref, skip_ref, w_ref, og_ref,
     gated_ref, qg_ref, kg_ref, vg_ref, fg_ref, sg_ref,
     og_all, w_all, table_f, table_b, fl_ref, inner_ext, inner_rev,
     acc_ref, mixed_ref, grad_ext, ig_ref, part_ref, got_ref, red_ref, all_ref,
     w_sem, own_sem, y_send, y_recv, core_send, core_recv, fwd_send, fwd_recv,
     rim_send, rim_recv, up_send, up_recv, p1_send, p1_recv, p2_send, p2_recv) = refs
    tok, chan = q_ref.shape
    groups, taps = f_ref.shape
    gsize = chan // groups
    per_tile = LANES // gsize
    tiles = chan // LANES
    kb = og_ref.shape[1]
    n_pieces = kb // PIECE
    n_chips = n_ch // 2

    ctx = lax.axis_index("ctx")
    ch = lax.axis_index("ch")
    chip, core = ch // 2, ch % 2
    sibling = chip * 2 + (1 - core)
    first, last = ctx == 0, ctx == n_ctx - 1

    barrier = pltpu.get_barrier_semaphore()
    if reduce_here:
        offsets = list(range(1, n_ctx))
    else:
        offsets = sorted({1, n_ctx - 1})
    for d in offsets:
        pl.semaphore_signal(barrier, inc=1, device_id={"ctx": lax.rem(ctx + d, n_ctx)}, device_id_type=MESH)
    pl.semaphore_signal(barrier, inc=1, device_id={"ch": sibling}, device_id_type=MESH)
    for d in range(1, n_chips):
        other = lax.rem(chip + d, n_chips) * 2 + core
        pl.semaphore_signal(barrier, inc=1, device_id={"ch": other}, device_id_type=MESH)

    def owner_of(index):
        if index == 0:
            return ch
        if index == 1:
            return sibling
        d, other = (index - 2) // 2 + 1, (index - 2) % 2
        base = lax.rem(chip - d + n_chips, n_chips) * 2
        return base + (core if other == 0 else 1 - core)

    def w_copy(index):
        cols = pl.ds(pl.multiple_of(owner_of(index) * kb, LANES), kb)
        return pltpu.make_async_copy(w_ref.at[:, cols], w_all.at[index], w_sem.at[index])

    own_copy = pltpu.make_async_copy(og_ref, og_all.at[ch], own_sem)
    own_copy.start()
    for index in range(n_ch):
        w_copy(index).start()

    pl.semaphore_wait(barrier, len(offsets) + 1 + n_chips - 1)

    def y_copy(d, p):
        cols = pl.ds(p * PIECE, PIECE)
        other = lax.rem(chip + d, n_chips) * 2 + core
        return pltpu.make_async_remote_copy(
            og_ref.at[:, cols], og_all.at[ch, :, cols], y_send.at[d - 1, p], y_recv.at[d - 1, p],
            device_id={"ch": other}, device_id_type=MESH)

    def fwd_copy(d, p):
        cols = pl.ds(p * PIECE, PIECE)
        owner = lax.rem(chip - d + n_chips, n_chips) * 2 + core
        piece = og_all.at[owner, :, cols]
        return pltpu.make_async_remote_copy(
            piece, piece, fwd_send.at[d - 1, p], fwd_recv.at[d - 1, p],
            device_id={"ch": sibling}, device_id_type=MESH)

    core_copy = pltpu.make_async_remote_copy(
        og_ref, og_all.at[ch], core_send, core_recv, device_id={"ch": sibling}, device_id_type=MESH)
    for p in range(n_pieces):
        for d in range(1, n_chips):
            y_copy(d, p).start()
    core_copy.start()

    inner_ext[tok:, :] = (k_ref[...].astype(F32) * v_ref[...].astype(F32)).astype(BF16)

    def rim_copy():
        return pltpu.make_async_remote_copy(
            inner_ext.at[pl.ds(tok, tok)], inner_ext.at[pl.ds(0, tok)], rim_send, rim_recv,
            device_id={"ctx": lax.rem(ctx + 1, n_ctx)}, device_id_type=MESH)

    @pl.when(jnp.logical_not(last))
    def _():
        rim_copy().start()

    @pl.when(first)
    def _():
        inner_ext[:tok, :] = jnp.zeros((tok, chan), BF16)

    @pl.when(last)
    def _():
        grad_ext[tok:, :] = jnp.zeros((tok, chan), BF16)

    row = lax.broadcasted_iota(jnp.int32, (tok, taps), 0)
    col = lax.broadcasted_iota(jnp.int32, (tok, taps), 1)
    negate = (lax.rem(row + col, taps) == 0).astype(BF16)
    flip = (row + col == taps - 1).astype(BF16)
    filt = f_ref[...]
    fl_ref[0] = filt.astype(F32)
    fl_ref[1] = jnp.dot(filt, negate, preferred_element_type=F32)

    def build(g, carry):
        rows = pl.ds(pl.multiple_of(g * tok, tok), tok)
        back = jnp.broadcast_to(fl_ref[0, pl.ds(g, 1), :], (tok, taps))
        back = pltpu.roll(back, 0, 1, stride=1, stride_axis=0)
        table_b[rows, :taps] = jnp.where(col >= row, back, 0.0).astype(BF16)
        table_b[rows, taps:] = jnp.where(col < row, back, 0.0).astype(BF16)
        fwd = jnp.broadcast_to(fl_ref[1, pl.ds(g, 1), :], (tok, taps))
        fwd = pltpu.roll(fwd, 0, 1, stride=1, stride_axis=0)
        table_f[rows, :taps] = jnp.where(col > row, fwd, 0.0).astype(BF16)
        table_f[rows, taps:] = jnp.where(col <= row, fwd, 0.0).astype(BF16)
        return carry

    lax.fori_loop(0, groups, build, 0)

    def multiply(index, owner, p, fresh=False):
        cols = pl.ds(pl.multiple_of(p * PIECE, PIECE), PIECE)
        product = lax.dot_general(
            w_all[index, :, cols], og_all[owner, :, cols], NT, preferred_element_type=F32)
        acc_ref[...] += product

    def multiply_block(index, owner):
        lax.fori_loop(0, n_pieces, lambda p, c: (multiply(index, owner, p), c)[1], 0)

    acc_ref[...] = jnp.zeros_like(acc_ref)
    own_copy.wait()
    w_copy(0).wait()
    multiply_block(0, ch)
    core_copy.wait_recv()
    w_copy(1).wait()
    multiply_block(1, sibling)

    lane_group = lax.broadcasted_iota(jnp.int32, (tok, LANES), 1) // gsize

    def pick(result):
        out = result[:tok]
        for i in range(1, per_tile):
            out = jnp.where(lane_group == i, result[i * tok:(i + 1) * tok], out)
        return out

    def tile_rows(k):
        return pl.ds(pl.multiple_of(k * per_tile * tok, per_tile * tok), per_tile * tok)

    def tile_lanes(k):
        return pl.ds(pl.multiple_of(k * LANES, LANES), LANES)

    @pl.when(jnp.logical_not(first))
    def _():
        rim_copy().wait_recv()

    def forward(k, carry):
        lanes = tile_lanes(k)
        result = jnp.dot(table_f[tile_rows(k), :], inner_ext[:, lanes], preferred_element_type=F32)
        mixed = pick(result) + skip_ref[:, lanes] * inner_ext[tok:, lanes].astype(F32)
        mixed_ref[:, lanes] = mixed
        gated_ref[:, lanes] = (q_ref[:, lanes].astype(F32) * mixed).astype(BF16)
        inner_rev[:tok, lanes] = jnp.dot(flip, inner_ext[:tok, lanes], preferred_element_type=F32).astype(BF16)
        inner_rev[tok:, lanes] = jnp.dot(flip, inner_ext[tok:, lanes], preferred_element_type=F32).astype(BF16)
        return carry

    lax.fori_loop(0, tiles, forward, 0)

    for index in range(2, n_ch):
        w_copy(index).wait()
    for p in range(n_pieces):
        for d in range(1, n_chips):
            y_copy(d, p).wait_recv()
            fwd_copy(d, p).start()
            multiply(2 * d, owner_of(2 * d), p)
            if p > 0:
                fwd_copy(d, p - 1).wait_recv()
                multiply(2 * d + 1, owner_of(2 * d + 1), p - 1)
    for d in range(1, n_chips):
        fwd_copy(d, n_pieces - 1).wait_recv()
        multiply(2 * d + 1, owner_of(2 * d + 1), n_pieces - 1)

    def up_copy(k):
        lanes = pl.ds(k * LANES, LANES)
        return pltpu.make_async_remote_copy(
            grad_ext.at[pl.ds(0, tok), lanes], grad_ext.at[pl.ds(tok, tok), lanes],
            up_send.at[k], up_recv.at[k],
            device_id={"ctx": lax.rem(ctx + n_ctx - 1, n_ctx)}, device_id_type=MESH)

    for k in range(tiles):
        lanes = pl.ds(k * LANES, LANES)
        mg = acc_ref[k * LANES:(k + 1) * LANES, :].T
        grad_ext[:tok, lanes] = (mg * q_ref[:, lanes].astype(F32)).astype(BF16)

        @pl.when(jnp.logical_not(first))
        def _():
            up_copy(k).start()

        qg_ref[:, lanes] = (mg * mixed_ref[:, lanes]).astype(BF16)

    def gradients(k, carry):
        lanes = tile_lanes(k)
        cg = grad_ext[:tok, lanes]
        zero = jnp.zeros_like(cg)
        masked = jnp.concatenate([jnp.where(lane_group == i, cg, zero) for i in range(per_tile)], axis=0)
        pairs = lax.dot_general(masked, inner_rev[:, lanes], NT, preferred_element_type=F32)
        sums = []
        for i in range(per_tile):
            block = pairs[i * tok:(i + 1) * tok]
            block = jnp.where(row + col >= taps - 1, block[:, taps:], block[:, :taps])
            block = pltpu.roll(block, 1, 1, stride=1, stride_axis=0)
            sums.append(jnp.sum(block, axis=0, keepdims=True))
        part_ref[k, :per_tile, :] = jnp.concatenate(sums, axis=0)
        skip = jnp.sum(cg.astype(F32) * inner_ext[tok:, lanes].astype(F32), axis=0, keepdims=True)
        part_ref[k, per_tile:, :] = jnp.broadcast_to(skip, (per_tile, LANES))
        return carry

    lax.fori_loop(0, tiles, gradients, 0)

    def p1_copy(d):
        target = lax.rem(ctx + d, n_ctx)
        return pltpu.make_async_remote_copy(
            part_ref.at[target], got_ref.at[d], p1_send.at[d], p1_recv.at[d],
            device_id={"ctx": target}, device_id_type=MESH)

    def p2_copy(d):
        target = lax.rem(ctx + d, n_ctx)
        return pltpu.make_async_remote_copy(
            red_ref, all_ref.at[ctx], p2_send.at[d], p2_recv.at[d],
            device_id={"ctx": target}, device_id_type=MESH)

    if reduce_here:
        for d in range(1, n_ctx):
            p1_copy(d).start()

    def backward(k, carry):
        lanes = tile_lanes(k)
        cg = grad_ext[:tok, lanes]
        result = jnp.dot(table_b[tile_rows(k), :taps], cg, preferred_element_type=F32)
        ig_ref[:, lanes] = pick(result) + skip_ref[:, lanes] * cg.astype(F32)
        return carry

    lax.fori_loop(0, tiles, backward, 0)

    if reduce_here:
        total = part_ref[ctx]
        for d in range(1, n_ctx):
            p1_copy(d).wait_recv()
            total = total + got_ref[d]
        red_ref[...] = total
        for d in range(1, n_ctx):
            p2_copy(d).start()

    for k in range(tiles):
        lanes = pl.ds(k * LANES, LANES)

        @pl.when(jnp.logical_not(last))
        def _():
            up_copy(k).wait_recv()

        rows = pl.ds(k * per_tile * tok, per_tile * tok)
        result = jnp.dot(table_b[rows, taps:], grad_ext[tok:, lanes], preferred_element_type=F32)
        ig = ig_ref[:, lanes] + pick(result)
        kg_ref[:, lanes] = (ig * v_ref[:, lanes].astype(F32)).astype(BF16)
        vg_ref[:, lanes] = (ig * k_ref[:, lanes].astype(F32)).astype(BF16)

    def write_sums(k, values):
        fg_ref[k] = values[:per_tile]
        sg_ref[k] = values[per_tile:per_tile + 1]

    if reduce_here:
        all_ref[ctx] = red_ref[...]
        for d in range(1, n_ctx):
            p2_copy(d).wait_recv()
        for k in range(tiles):
            write_sums(k, all_ref[k])
        for d in range(1, n_ctx):
            p1_copy(d).wait_send()
            p2_copy(d).wait_send()
    else:
        for k in range(tiles):
            write_sums(k, part_ref[k])

    core_copy.wait_send()
    for p in range(n_pieces):
        for d in range(1, n_chips):
            y_copy(d, p).wait_send()
            fwd_copy(d, p).wait_send()

    @pl.when(jnp.logical_not(last))
    def _():
        rim_copy().wait_send()

    @pl.when(jnp.logical_not(first))
    def _():
        for k in range(tiles):
            up_copy(k).wait_send()


def per_device(n_ctx, n_ch, query_act, key_act, value_act, filters, skip_bias, out_weight, out_grad):
    tok, chan = query_act.shape
    groups, taps = filters.shape
    kb = out_grad.shape[1]
    tiles = chan // LANES
    per_tile = LANES * groups // chan
    n_pieces = kb // PIECE
    n_hops = max(n_ch // 2 - 1, 1)
    reduce_here = tiles == n_ctx
    dma = pltpu.SemaphoreType.DMA
    vmem = pl.BlockSpec(memory_space=pltpu.VMEM)
    hbm = pl.BlockSpec(memory_space=pl.ANY)
    n_slots = n_ctx if reduce_here else 1
    act = jax.ShapeDtypeStruct((tok, chan), BF16)
    outs = pl.pallas_call(
        functools.partial(kernel_body, n_ctx, n_ch, reduce_here),
        out_shape=(
            act, act, act, act,
            jax.ShapeDtypeStruct((tiles, per_tile, LANES), F32),
            jax.ShapeDtypeStruct((tiles, 1, LANES), F32),
        ),
        in_specs=[vmem] * 5 + [hbm] * 2,
        out_specs=(vmem,) * 6,
        scratch_shapes=[
            pltpu.VMEM((n_ch, tok, kb), BF16),
            pltpu.VMEM((n_ch, chan, kb), BF16),
            pltpu.VMEM((groups * tok, 2 * taps), BF16),
            pltpu.VMEM((groups * tok, 2 * taps), BF16),
            pltpu.VMEM((2, groups, taps), F32),
            pltpu.VMEM((2 * tok, chan), BF16),
            pltpu.VMEM((2 * tok, chan), BF16),
            pltpu.VMEM((chan, tok), F32),
            pltpu.VMEM((tok, chan), F32),
            pltpu.VMEM((2 * tok, chan), BF16),
            pltpu.VMEM((tok, chan), F32),
            pltpu.VMEM((tiles, 2 * per_tile, LANES), F32),
            pltpu.VMEM((n_slots, 2 * per_tile, LANES), F32),
            pltpu.VMEM((2 * per_tile, LANES), F32),
            pltpu.VMEM((n_slots, 2 * per_tile, LANES), F32),
            dma((n_ch,)), dma,
            dma((n_hops, n_pieces)), dma((n_hops, n_pieces)),
            dma, dma,
            dma((n_hops, n_pieces)), dma((n_hops, n_pieces)),
            dma, dma,
            dma((tiles,)), dma((tiles,)),
            dma((n_slots,)), dma((n_slots,)), dma((n_slots,)), dma((n_slots,)),
        ],
        compiler_params=pltpu.CompilerParams(
            collective_id=0, has_side_effects=True, vmem_limit_bytes=56 * 2**20),
        name="hyena",
    )(query_act, key_act, value_act, filters, skip_bias.reshape(1, chan), out_weight, out_grad)
    gated, query_grad, key_grad, value_grad, filter_grad, skip_grad = outs
    filter_grad = filter_grad.reshape(groups, taps)
    skip_grad = skip_grad.reshape(chan)
    if not reduce_here:
        filter_grad, skip_grad = lax.psum((filter_grad, skip_grad), "ctx")
    return gated, query_grad, key_grad, value_grad, filter_grad, skip_grad


def solution(mesh):
    act = P("ctx", "ch")
    in_specs = (act, act, act, P("ch", None), P("ch"), P("ch", None), act)
    out_specs = (act, act, act, act, P("ch", None), P("ch"))
    return jax.shard_map(
        functools.partial(per_device, mesh.shape["ctx"], mesh.shape["ch"]),
        mesh=mesh, in_specs=in_specs, out_specs=out_specs, check_vma=False,
    )
```

```python
import functools

import jax
import jax.numpy as jnp
from jax import lax
from jax.experimental import pallas as pl
from jax.experimental.pallas import tpu as pltpu
from jax.sharding import PartitionSpec as P

LANES = 128
PIECE = 1024
MESH = pl.DeviceIdType.MESH
F32 = jnp.float32
BF16 = jnp.bfloat16
NT = (((1,), (1,)), ((), ()))


def kernel_body(n_ctx, n_ch, reduce_here, *refs):
    (q_ref, k_ref, v_ref, f_ref, skip_ref, w_ref, og_ref,
     gated_ref, qg_ref, kg_ref, vg_ref, fg_ref, sg_ref,
     og_all, w_all, table_f, table_b, fl_ref, inner_ext, inner_rev,
     acc_ref, mixed_ref, grad_ext, ig_ref, part_ref, got_ref, red_ref, all_ref,
     w_sem, own_sem, y_send, y_recv, core_send, core_recv, fwd_send, fwd_recv,
     rim_send, rim_recv, up_send, up_recv, p1_send, p1_recv, p2_send, p2_recv) = refs
    tok, chan = q_ref.shape
    groups, taps = f_ref.shape
    gsize = chan // groups
    per_tile = LANES // gsize
    tiles = chan // LANES
    kb = og_ref.shape[1]
    n_pieces = kb // PIECE
    n_chips = n_ch // 2

    ctx = lax.axis_index("ctx")
    ch = lax.axis_index("ch")
    chip, core = ch // 2, ch % 2
    sibling = chip * 2 + (1 - core)
    first, last = ctx == 0, ctx == n_ctx - 1

    barrier = pltpu.get_barrier_semaphore()
    if reduce_here:
        offsets = list(range(1, n_ctx))
    else:
        offsets = sorted({1, n_ctx - 1})
    for d in offsets:
        pl.semaphore_signal(barrier, inc=1, device_id={"ctx": lax.rem(ctx + d, n_ctx)}, device_id_type=MESH)
    pl.semaphore_signal(barrier, inc=1, device_id={"ch": sibling}, device_id_type=MESH)
    for d in range(1, n_chips):
        other = lax.rem(chip + d, n_chips) * 2 + core
        pl.semaphore_signal(barrier, inc=1, device_id={"ch": other}, device_id_type=MESH)

    def owner_of(index):
        if index == 0:
            return ch
        if index == 1:
            return sibling
        d, other = (index - 2) // 2 + 1, (index - 2) % 2
        base = lax.rem(chip - d + n_chips, n_chips) * 2
        return base + (core if other == 0 else 1 - core)

    def w_copy(index):
        cols = pl.ds(pl.multiple_of(owner_of(index) * kb, LANES), kb)
        return pltpu.make_async_copy(w_ref.at[:, cols], w_all.at[index], w_sem.at[index])

    own_copy = pltpu.make_async_copy(og_ref, og_all.at[ch], own_sem)
    own_copy.start()
    for index in range(n_ch):
        w_copy(index).start()

    pl.semaphore_wait(barrier, len(offsets) + 1 + n_chips - 1)

    def y_copy(d, p):
        cols = pl.ds(p * PIECE, PIECE)
        other = lax.rem(chip + d, n_chips) * 2 + core
        return pltpu.make_async_remote_copy(
            og_ref.at[:, cols], og_all.at[ch, :, cols], y_send.at[d - 1, p], y_recv.at[d - 1, p],
            device_id={"ch": other}, device_id_type=MESH)

    def fwd_copy(d, p):
        cols = pl.ds(p * PIECE, PIECE)
        owner = lax.rem(chip - d + n_chips, n_chips) * 2 + core
        piece = og_all.at[owner, :, cols]
        return pltpu.make_async_remote_copy(
            piece, piece, fwd_send.at[d - 1, p], fwd_recv.at[d - 1, p],
            device_id={"ch": sibling}, device_id_type=MESH)

    core_copy = pltpu.make_async_remote_copy(
        og_ref, og_all.at[ch], core_send, core_recv, device_id={"ch": sibling}, device_id_type=MESH)
    for p in range(n_pieces):
        for d in range(1, n_chips):
            y_copy(d, p).start()
    core_copy.start()

    inner_ext[tok:, :] = (k_ref[...].astype(F32) * v_ref[...].astype(F32)).astype(BF16)

    def rim_copy():
        return pltpu.make_async_remote_copy(
            inner_ext.at[pl.ds(tok, tok)], inner_ext.at[pl.ds(0, tok)], rim_send, rim_recv,
            device_id={"ctx": lax.rem(ctx + 1, n_ctx)}, device_id_type=MESH)

    @pl.when(jnp.logical_not(last))
    def _():
        rim_copy().start()

    @pl.when(first)
    def _():
        inner_ext[:tok, :] = jnp.zeros((tok, chan), BF16)

    @pl.when(last)
    def _():
        grad_ext[tok:, :] = jnp.zeros((tok, chan), BF16)

    row = lax.broadcasted_iota(jnp.int32, (tok, taps), 0)
    col = lax.broadcasted_iota(jnp.int32, (tok, taps), 1)
    negate = (lax.rem(row + col, taps) == 0).astype(BF16)
    flip = (row + col == taps - 1).astype(BF16)
    filt = f_ref[...]
    fl_ref[0] = filt.astype(F32)
    fl_ref[1] = jnp.dot(filt, negate, preferred_element_type=F32)

    def build(g, carry):
        rows = pl.ds(pl.multiple_of(g * tok, tok), tok)
        fwd = jnp.broadcast_to(fl_ref[1, pl.ds(g, 1), :], (tok, taps))
        fwd = pltpu.roll(fwd, 0, 1, stride=1, stride_axis=0)
        table_f[rows, :taps] = jnp.where(col > row, fwd, 0.0).astype(BF16)
        table_f[rows, taps:] = jnp.where(col <= row, fwd, 0.0).astype(BF16)
        return carry

    lax.fori_loop(0, groups, build, 0)

    def build_back(g, carry):
        rows = pl.ds(pl.multiple_of(g * tok, tok), tok)
        back = jnp.broadcast_to(fl_ref[0, pl.ds(g, 1), :], (tok, taps))
        back = pltpu.roll(back, 0, 1, stride=1, stride_axis=0)
        table_b[rows, :taps] = jnp.where(col >= row, back, 0.0).astype(BF16)
        table_b[rows, taps:] = jnp.where(col < row, back, 0.0).astype(BF16)
        return carry

    def multiply(index, owner, p, fresh=False):
        cols = pl.ds(pl.multiple_of(p * PIECE, PIECE), PIECE)
        product = lax.dot_general(
            w_all[index, :, cols], og_all[owner, :, cols], NT, preferred_element_type=F32)
        acc_ref[...] += product

    def multiply_block(index, owner):
        lax.fori_loop(0, n_pieces, lambda p, c: (multiply(index, owner, p), c)[1], 0)

    acc_ref[...] = jnp.zeros_like(acc_ref)
    own_copy.wait()
    w_copy(0).wait()
    multiply_block(0, ch)
    core_copy.wait_recv()
    w_copy(1).wait()
    multiply_block(1, sibling)

    lane_group = lax.broadcasted_iota(jnp.int32, (tok, LANES), 1) // gsize

    def pick(result):
        out = result[:tok]
        for i in range(1, per_tile):
            out = jnp.where(lane_group == i, result[i * tok:(i + 1) * tok], out)
        return out

    def tile_rows(k):
        return pl.ds(pl.multiple_of(k * per_tile * tok, per_tile * tok), per_tile * tok)

    def tile_lanes(k):
        return pl.ds(pl.multiple_of(k * LANES, LANES), LANES)

    @pl.when(jnp.logical_not(first))
    def _():
        rim_copy().wait_recv()

    def forward(k, carry):
        lanes = tile_lanes(k)
        result = jnp.dot(table_f[tile_rows(k), :], inner_ext[:, lanes], preferred_element_type=F32)
        mixed = pick(result) + skip_ref[:, lanes] * inner_ext[tok:, lanes].astype(F32)
        mixed_ref[:, lanes] = mixed
        gated_ref[:, lanes] = (q_ref[:, lanes].astype(F32) * mixed).astype(BF16)
        inner_rev[:tok, lanes] = jnp.dot(flip, inner_ext[:tok, lanes], preferred_element_type=F32).astype(BF16)
        inner_rev[tok:, lanes] = jnp.dot(flip, inner_ext[tok:, lanes], preferred_element_type=F32).astype(BF16)
        return carry

    lax.fori_loop(0, tiles, forward, 0)

    for index in range(2, n_ch):
        w_copy(index).wait()
    for p in range(n_pieces):
        for d in range(1, n_chips):
            y_copy(d, p).wait_recv()
            fwd_copy(d, p).start()
            multiply(2 * d, owner_of(2 * d), p)
            if p > 0:
                fwd_copy(d, p - 1).wait_recv()
                multiply(2 * d + 1, owner_of(2 * d + 1), p - 1)
    for d in range(1, n_chips):
        fwd_copy(d, n_pieces - 1).wait_recv()
        multiply(2 * d + 1, owner_of(2 * d + 1), n_pieces - 1)

    def up_copy(k):
        lanes = pl.ds(k * LANES, LANES)
        return pltpu.make_async_remote_copy(
            grad_ext.at[pl.ds(0, tok), lanes], grad_ext.at[pl.ds(tok, tok), lanes],
            up_send.at[k], up_recv.at[k],
            device_id={"ctx": lax.rem(ctx + n_ctx - 1, n_ctx)}, device_id_type=MESH)

    for k in range(tiles):
        lanes = pl.ds(k * LANES, LANES)
        mg = acc_ref[k * LANES:(k + 1) * LANES, :].T
        grad_ext[:tok, lanes] = (mg * q_ref[:, lanes].astype(F32)).astype(BF16)

        @pl.when(jnp.logical_not(first))
        def _():
            up_copy(k).start()

        qg_ref[:, lanes] = (mg * mixed_ref[:, lanes]).astype(BF16)

    def gradients(k, carry):
        lanes = tile_lanes(k)
        cg = grad_ext[:tok, lanes]
        zero = jnp.zeros_like(cg)
        masked = jnp.concatenate([jnp.where(lane_group == i, cg, zero) for i in range(per_tile)], axis=0)
        pairs = lax.dot_general(masked, inner_rev[:, lanes], NT, preferred_element_type=F32)
        sums = []
        for i in range(per_tile):
            block = pairs[i * tok:(i + 1) * tok]
            block = jnp.where(row + col >= taps - 1, block[:, taps:], block[:, :taps])
            block = pltpu.roll(block, 1, 1, stride=1, stride_axis=0)
            sums.append(jnp.sum(block, axis=0, keepdims=True))
        part_ref[k, :per_tile, :] = jnp.concatenate(sums, axis=0)
        skip = jnp.sum(cg.astype(F32) * inner_ext[tok:, lanes].astype(F32), axis=0, keepdims=True)
        part_ref[k, per_tile:, :] = jnp.broadcast_to(skip, (per_tile, LANES))
        return carry

    lax.fori_loop(0, tiles, gradients, 0)

    def p1_copy(d):
        target = lax.rem(ctx + d, n_ctx)
        return pltpu.make_async_remote_copy(
            part_ref.at[target], got_ref.at[d], p1_send.at[d], p1_recv.at[d],
            device_id={"ctx": target}, device_id_type=MESH)

    def p2_copy(d):
        target = lax.rem(ctx + d, n_ctx)
        return pltpu.make_async_remote_copy(
            red_ref, all_ref.at[ctx], p2_send.at[d], p2_recv.at[d],
            device_id={"ctx": target}, device_id_type=MESH)

    if reduce_here:
        for d in range(1, n_ctx):
            p1_copy(d).start()

    lax.fori_loop(0, groups, build_back, 0)

    def backward(k, carry):
        lanes = tile_lanes(k)
        cg = grad_ext[:tok, lanes]
        result = jnp.dot(table_b[tile_rows(k), :taps], cg, preferred_element_type=F32)
        ig_ref[:, lanes] = pick(result) + skip_ref[:, lanes] * cg.astype(F32)
        return carry

    lax.fori_loop(0, tiles, backward, 0)

    if reduce_here:
        total = part_ref[ctx]
        for d in range(1, n_ctx):
            p1_copy(d).wait_recv()
            total = total + got_ref[d]
        red_ref[...] = total
        for d in range(1, n_ctx):
            p2_copy(d).start()

    for k in range(tiles):
        lanes = pl.ds(k * LANES, LANES)

        @pl.when(jnp.logical_not(last))
        def _():
            up_copy(k).wait_recv()

        rows = pl.ds(k * per_tile * tok, per_tile * tok)
        result = jnp.dot(table_b[rows, taps:], grad_ext[tok:, lanes], preferred_element_type=F32)
        ig = ig_ref[:, lanes] + pick(result)
        kg_ref[:, lanes] = (ig * v_ref[:, lanes].astype(F32)).astype(BF16)
        vg_ref[:, lanes] = (ig * k_ref[:, lanes].astype(F32)).astype(BF16)

    def write_sums(k, values):
        fg_ref[k] = values[:per_tile]
        sg_ref[k] = values[per_tile:per_tile + 1]

    if reduce_here:
        all_ref[ctx] = red_ref[...]
        for d in range(1, n_ctx):
            p2_copy(d).wait_recv()
        for k in range(tiles):
            write_sums(k, all_ref[k])
        for d in range(1, n_ctx):
            p1_copy(d).wait_send()
            p2_copy(d).wait_send()
    else:
        for k in range(tiles):
            write_sums(k, part_ref[k])

    core_copy.wait_send()
    for p in range(n_pieces):
        for d in range(1, n_chips):
            y_copy(d, p).wait_send()
            fwd_copy(d, p).wait_send()

    @pl.when(jnp.logical_not(last))
    def _():
        rim_copy().wait_send()

    @pl.when(jnp.logical_not(first))
    def _():
        for k in range(tiles):
            up_copy(k).wait_send()


def hand_on(*refs):
    count = (len(refs) - 1) // 2
    copies = [
        pltpu.make_async_copy(refs[i], refs[count + i], refs[-1].at[i]) for i in range(count)
    ]
    for copy in copies:
        copy.start()
    for copy in copies:
        copy.wait()


def per_device(n_ctx, n_ch, query_act, key_act, value_act, filters, skip_bias, out_weight, out_grad):
    tok, chan = query_act.shape
    groups, taps = filters.shape
    kb = out_grad.shape[1]
    tiles = chan // LANES
    per_tile = LANES * groups // chan
    n_pieces = kb // PIECE
    n_hops = max(n_ch // 2 - 1, 1)
    reduce_here = tiles == n_ctx
    dma = pltpu.SemaphoreType.DMA
    vmem = pl.BlockSpec(memory_space=pltpu.VMEM)
    hbm = pl.BlockSpec(memory_space=pl.ANY)
    n_slots = n_ctx if reduce_here else 1
    act = jax.ShapeDtypeStruct((tok, chan), BF16)
    outs = pl.pallas_call(
        functools.partial(kernel_body, n_ctx, n_ch, reduce_here),
        out_shape=(
            act, act, act, act,
            jax.ShapeDtypeStruct((tiles, per_tile, LANES), F32),
            jax.ShapeDtypeStruct((tiles, 1, LANES), F32),
        ),
        in_specs=[vmem] * 5 + [hbm] * 2,
        out_specs=(vmem,) * 6,
        scratch_shapes=[
            pltpu.VMEM((n_ch, tok, kb), BF16),
            pltpu.VMEM((n_ch, chan, kb), BF16),
            pltpu.VMEM((groups * tok, 2 * taps), BF16),
            pltpu.VMEM((groups * tok, 2 * taps), BF16),
            pltpu.VMEM((2, groups, taps), F32),
            pltpu.VMEM((2 * tok, chan), BF16),
            pltpu.VMEM((2 * tok, chan), BF16),
            pltpu.VMEM((chan, tok), F32),
            pltpu.VMEM((tok, chan), F32),
            pltpu.VMEM((2 * tok, chan), BF16),
            pltpu.VMEM((tok, chan), F32),
            pltpu.VMEM((tiles, 2 * per_tile, LANES), F32),
            pltpu.VMEM((n_slots, 2 * per_tile, LANES), F32),
            pltpu.VMEM((2 * per_tile, LANES), F32),
            pltpu.VMEM((n_slots, 2 * per_tile, LANES), F32),
            dma((n_ch,)), dma,
            dma((n_hops, n_pieces)), dma((n_hops, n_pieces)),
            dma, dma,
            dma((n_hops, n_pieces)), dma((n_hops, n_pieces)),
            dma, dma,
            dma((tiles,)), dma((tiles,)),
            dma((n_slots,)), dma((n_slots,)), dma((n_slots,)), dma((n_slots,)),
        ],
        compiler_params=pltpu.CompilerParams(
            collective_id=0, has_side_effects=True, vmem_limit_bytes=56 * 2**20),
        name="hyena",
    )(query_act, key_act, value_act, filters, skip_bias.reshape(1, chan), out_weight, out_grad)
    outs = pl.pallas_call(
        hand_on,
        out_shape=tuple(jax.ShapeDtypeStruct(x.shape, x.dtype) for x in outs),
        in_specs=[vmem] * len(outs),
        out_specs=(hbm,) * len(outs),
        scratch_shapes=[dma((len(outs),))],
        name="hand_on",
    )(*outs)
    gated, query_grad, key_grad, value_grad, filter_grad, skip_grad = outs
    filter_grad = filter_grad.reshape(groups, taps)
    skip_grad = skip_grad.reshape(chan)
    if not reduce_here:
        filter_grad, skip_grad = lax.psum((filter_grad, skip_grad), "ctx")
    return gated, query_grad, key_grad, value_grad, filter_grad, skip_grad


def solution(mesh):
    act = P("ctx", "ch")
    in_specs = (act, act, act, P("ch", None), P("ch"), P("ch", None), act)
    out_specs = (act, act, act, act, P("ch", None), P("ch"))
    return jax.shard_map(
        functools.partial(per_device, mesh.shape["ctx"], mesh.shape["ch"]),
        mesh=mesh, in_specs=in_specs, out_specs=out_specs, check_vma=False,
    )
```

```python
import functools

import jax
import jax.numpy as jnp
from jax import lax
from jax.experimental import pallas as pl
from jax.experimental.pallas import tpu as pltpu
from jax.sharding import PartitionSpec as P

LANES = 128
PIECE = 1024
MESH = pl.DeviceIdType.MESH
F32 = jnp.float32
BF16 = jnp.bfloat16
NT = (((1,), (1,)), ((), ()))


def kernel_body(n_ctx, n_ch, reduce_here, *refs):
    (q_ref, k_ref, v_ref, f_ref, skip_ref, w_ref, og_ref,
     gated_ref, qg_ref, kg_ref, vg_ref, fg_ref, sg_ref,
     og_all, w_all, table_f, table_b, fl_ref, inner_ext, inner_rev,
     acc_ref, mixed_ref, grad_ext, ig_ref, part_ref, got_ref, red_ref, all_ref,
     w_sem, own_sem, y_send, y_recv, core_send, core_recv, fwd_send, fwd_recv,
     rim_send, rim_recv, up_send, up_recv, p1_send, p1_recv, p2_send, p2_recv) = refs
    tok, chan = q_ref.shape
    groups, taps = f_ref.shape
    gsize = chan // groups
    per_tile = LANES // gsize
    tiles = chan // LANES
    kb = og_ref.shape[1]
    n_pieces = kb // PIECE
    n_chips = n_ch // 2

    ctx = lax.axis_index("ctx")
    ch = lax.axis_index("ch")
    chip, core = ch // 2, ch % 2
    sibling = chip * 2 + (1 - core)
    first, last = ctx == 0, ctx == n_ctx - 1

    barrier = pltpu.get_barrier_semaphore()
    if reduce_here:
        offsets = list(range(1, n_ctx))
    else:
        offsets = sorted({1, n_ctx - 1})
    for d in offsets:
        pl.semaphore_signal(barrier, inc=1, device_id={"ctx": lax.rem(ctx + d, n_ctx)}, device_id_type=MESH)
    pl.semaphore_signal(barrier, inc=1, device_id={"ch": sibling}, device_id_type=MESH)
    for d in range(1, n_chips):
        other = lax.rem(chip + d, n_chips) * 2 + core
        pl.semaphore_signal(barrier, inc=1, device_id={"ch": other}, device_id_type=MESH)

    def owner_of(index):
        if index == 0:
            return ch
        if index == 1:
            return sibling
        d, other = (index - 2) // 2 + 1, (index - 2) % 2
        base = lax.rem(chip - d + n_chips, n_chips) * 2
        return base + (core if other == 0 else 1 - core)

    def w_copy(index):
        cols = pl.ds(pl.multiple_of(owner_of(index) * kb, LANES), kb)
        return pltpu.make_async_copy(w_ref.at[:, cols], w_all.at[index], w_sem.at[index])

    own_copy = pltpu.make_async_copy(og_ref, og_all.at[ch], own_sem)
    own_copy.start()
    for index in range(n_ch):
        w_copy(index).start()

    inner_ext[tok:, :] = (k_ref[...].astype(F32) * v_ref[...].astype(F32)).astype(BF16)
    @pl.when(first)
    def _():
        inner_ext[:tok, :] = jnp.zeros((tok, chan), BF16)

    @pl.when(last)
    def _():
        grad_ext[tok:, :] = jnp.zeros((tok, chan), BF16)

    row = lax.broadcasted_iota(jnp.int32, (tok, taps), 0)
    col = lax.broadcasted_iota(jnp.int32, (tok, taps), 1)
    negate = (lax.rem(row + col, taps) == 0).astype(BF16)
    flip = (row + col == taps - 1).astype(BF16)
    filt = f_ref[...]
    fl_ref[0] = filt.astype(F32)
    fl_ref[1] = jnp.dot(filt, negate, preferred_element_type=F32)
    acc_ref[...] = jnp.zeros_like(acc_ref)

    pl.semaphore_wait(barrier, len(offsets) + 1 + n_chips - 1)

    def y_copy(d, p):
        cols = pl.ds(p * PIECE, PIECE)
        other = lax.rem(chip + d, n_chips) * 2 + core
        return pltpu.make_async_remote_copy(
            og_ref.at[:, cols], og_all.at[ch, :, cols], y_send.at[d - 1, p], y_recv.at[d - 1, p],
            device_id={"ch": other}, device_id_type=MESH)

    def fwd_copy(d, p):
        cols = pl.ds(p * PIECE, PIECE)
        owner = lax.rem(chip - d + n_chips, n_chips) * 2 + core
        piece = og_all.at[owner, :, cols]
        return pltpu.make_async_remote_copy(
            piece, piece, fwd_send.at[d - 1, p], fwd_recv.at[d - 1, p],
            device_id={"ch": sibling}, device_id_type=MESH)

    core_copy = pltpu.make_async_remote_copy(
        og_ref, og_all.at[ch], core_send, core_recv, device_id={"ch": sibling}, device_id_type=MESH)
    for p in range(n_pieces):
        for d in range(1, n_chips):
            y_copy(d, p).start()
    core_copy.start()


    def rim_copy():
        return pltpu.make_async_remote_copy(
            inner_ext.at[pl.ds(tok, tok)], inner_ext.at[pl.ds(0, tok)], rim_send, rim_recv,
            device_id={"ctx": lax.rem(ctx + 1, n_ctx)}, device_id_type=MESH)

    @pl.when(jnp.logical_not(last))
    def _():
        rim_copy().start()

    def build(g, carry):
        rows = pl.ds(pl.multiple_of(g * tok, tok), tok)
        fwd = jnp.broadcast_to(fl_ref[1, pl.ds(g, 1), :], (tok, taps))
        fwd = pltpu.roll(fwd, 0, 1, stride=1, stride_axis=0)
        table_f[rows, :taps] = jnp.where(col > row, fwd, 0.0).astype(BF16)
        table_f[rows, taps:] = jnp.where(col <= row, fwd, 0.0).astype(BF16)
        return carry

    lax.fori_loop(0, groups, build, 0)

    def build_back(g, carry):
        rows = pl.ds(pl.multiple_of(g * tok, tok), tok)
        back = jnp.broadcast_to(fl_ref[0, pl.ds(g, 1), :], (tok, taps))
        back = pltpu.roll(back, 0, 1, stride=1, stride_axis=0)
        table_b[rows, :taps] = jnp.where(col >= row, back, 0.0).astype(BF16)
        table_b[rows, taps:] = jnp.where(col < row, back, 0.0).astype(BF16)
        return carry

    def multiply(index, owner, p, fresh=False):
        cols = pl.ds(pl.multiple_of(p * PIECE, PIECE), PIECE)
        product = lax.dot_general(
            w_all[index, :, cols], og_all[owner, :, cols], NT, preferred_element_type=F32)
        acc_ref[...] += product

    def multiply_block(index, owner):
        lax.fori_loop(0, n_pieces, lambda p, c: (multiply(index, owner, p), c)[1], 0)

    own_copy.wait()
    w_copy(0).wait()
    multiply_block(0, ch)
    core_copy.wait_recv()
    w_copy(1).wait()
    multiply_block(1, sibling)

    lane_group = lax.broadcasted_iota(jnp.int32, (tok, LANES), 1) // gsize

    def pick(result):
        out = result[:tok]
        for i in range(1, per_tile):
            out = jnp.where(lane_group == i, result[i * tok:(i + 1) * tok], out)
        return out

    def tile_rows(k):
        return pl.ds(pl.multiple_of(k * per_tile * tok, per_tile * tok), per_tile * tok)

    def tile_lanes(k):
        return pl.ds(pl.multiple_of(k * LANES, LANES), LANES)

    @pl.when(jnp.logical_not(first))
    def _():
        rim_copy().wait_recv()

    def forward(k, carry):
        lanes = tile_lanes(k)
        result = jnp.dot(table_f[tile_rows(k), :], inner_ext[:, lanes], preferred_element_type=F32)
        mixed = pick(result) + skip_ref[:, lanes] * inner_ext[tok:, lanes].astype(F32)
        mixed_ref[:, lanes] = mixed
        gated_ref[:, lanes] = (q_ref[:, lanes].astype(F32) * mixed).astype(BF16)
        inner_rev[:tok, lanes] = jnp.dot(flip, inner_ext[:tok, lanes], preferred_element_type=F32).astype(BF16)
        inner_rev[tok:, lanes] = jnp.dot(flip, inner_ext[tok:, lanes], preferred_element_type=F32).astype(BF16)
        return carry

    lax.fori_loop(0, tiles, forward, 0)

    for index in range(2, n_ch):
        w_copy(index).wait()
    for p in range(n_pieces):
        for d in range(1, n_chips):
            y_copy(d, p).wait_recv()
            fwd_copy(d, p).start()
            multiply(2 * d, owner_of(2 * d), p)
            if p > 0:
                fwd_copy(d, p - 1).wait_recv()
                multiply(2 * d + 1, owner_of(2 * d + 1), p - 1)
    for d in range(1, n_chips):
        fwd_copy(d, n_pieces - 1).wait_recv()
        multiply(2 * d + 1, owner_of(2 * d + 1), n_pieces - 1)

    def up_copy(k):
        lanes = pl.ds(k * LANES, LANES)
        return pltpu.make_async_remote_copy(
            grad_ext.at[pl.ds(0, tok), lanes], grad_ext.at[pl.ds(tok, tok), lanes],
            up_send.at[k], up_recv.at[k],
            device_id={"ctx": lax.rem(ctx + n_ctx - 1, n_ctx)}, device_id_type=MESH)

    for k in range(tiles):
        lanes = pl.ds(k * LANES, LANES)
        mg = acc_ref[k * LANES:(k + 1) * LANES, :].T
        grad_ext[:tok, lanes] = (mg * q_ref[:, lanes].astype(F32)).astype(BF16)

        @pl.when(jnp.logical_not(first))
        def _():
            up_copy(k).start()

        qg_ref[:, lanes] = (mg * mixed_ref[:, lanes]).astype(BF16)

    def gradients(k, carry):
        lanes = tile_lanes(k)
        cg = grad_ext[:tok, lanes]
        zero = jnp.zeros_like(cg)
        masked = jnp.concatenate([jnp.where(lane_group == i, cg, zero) for i in range(per_tile)], axis=0)
        pairs = lax.dot_general(masked, inner_rev[:, lanes], NT, preferred_element_type=F32)
        sums = []
        for i in range(per_tile):
            block = pairs[i * tok:(i + 1) * tok]
            block = jnp.where(row + col >= taps - 1, block[:, taps:], block[:, :taps])
            block = pltpu.roll(block, 1, 1, stride=1, stride_axis=0)
            sums.append(jnp.sum(block, axis=0, keepdims=True))
        part_ref[k, :per_tile, :] = jnp.concatenate(sums, axis=0)
        skip = jnp.sum(cg.astype(F32) * inner_ext[tok:, lanes].astype(F32), axis=0, keepdims=True)
        part_ref[k, per_tile:, :] = jnp.broadcast_to(skip, (per_tile, LANES))
        return carry

    lax.fori_loop(0, tiles, gradients, 0)

    def p1_copy(d):
        target = lax.rem(ctx + d, n_ctx)
        return pltpu.make_async_remote_copy(
            part_ref.at[target], got_ref.at[d], p1_send.at[d], p1_recv.at[d],
            device_id={"ctx": target}, device_id_type=MESH)

    def p2_copy(d):
        target = lax.rem(ctx + d, n_ctx)
        return pltpu.make_async_remote_copy(
            red_ref, all_ref.at[ctx], p2_send.at[d], p2_recv.at[d],
            device_id={"ctx": target}, device_id_type=MESH)

    if reduce_here:
        for d in range(1, n_ctx):
            p1_copy(d).start()

    lax.fori_loop(0, groups, build_back, 0)

    def backward(k, carry):
        lanes = tile_lanes(k)
        cg = grad_ext[:tok, lanes]
        result = jnp.dot(table_b[tile_rows(k), :taps], cg, preferred_element_type=F32)
        ig_ref[:, lanes] = pick(result) + skip_ref[:, lanes] * cg.astype(F32)
        return carry

    lax.fori_loop(0, tiles, backward, 0)

    if reduce_here:
        total = part_ref[ctx]
        for d in range(1, n_ctx):
            p1_copy(d).wait_recv()
            total = total + got_ref[d]
        red_ref[...] = total
        for d in range(1, n_ctx):
            p2_copy(d).start()

    for k in range(tiles):
        lanes = pl.ds(k * LANES, LANES)

        @pl.when(jnp.logical_not(last))
        def _():
            up_copy(k).wait_recv()

        rows = pl.ds(k * per_tile * tok, per_tile * tok)
        result = jnp.dot(table_b[rows, taps:], grad_ext[tok:, lanes], preferred_element_type=F32)
        ig = ig_ref[:, lanes] + pick(result)
        kg_ref[:, lanes] = (ig * v_ref[:, lanes].astype(F32)).astype(BF16)
        vg_ref[:, lanes] = (ig * k_ref[:, lanes].astype(F32)).astype(BF16)

    def write_sums(k, values):
        fg_ref[k] = values[:per_tile]
        sg_ref[k] = values[per_tile:per_tile + 1]

    if reduce_here:
        all_ref[ctx] = red_ref[...]
        for d in range(1, n_ctx):
            p2_copy(d).wait_recv()
        for k in range(tiles):
            write_sums(k, all_ref[k])
        for d in range(1, n_ctx):
            p1_copy(d).wait_send()
            p2_copy(d).wait_send()
    else:
        for k in range(tiles):
            write_sums(k, part_ref[k])

    core_copy.wait_send()
    for p in range(n_pieces):
        for d in range(1, n_chips):
            y_copy(d, p).wait_send()
            fwd_copy(d, p).wait_send()

    @pl.when(jnp.logical_not(last))
    def _():
        rim_copy().wait_send()

    @pl.when(jnp.logical_not(first))
    def _():
        for k in range(tiles):
            up_copy(k).wait_send()


def hand_on(*refs):
    count = (len(refs) - 1) // 2
    copies = [
        pltpu.make_async_copy(refs[i], refs[count + i], refs[-1].at[i]) for i in range(count)
    ]
    for copy in copies:
        copy.start()
    for copy in copies:
        copy.wait()


def per_device(n_ctx, n_ch, query_act, key_act, value_act, filters, skip_bias, out_weight, out_grad):
    tok, chan = query_act.shape
    groups, taps = filters.shape
    kb = out_grad.shape[1]
    tiles = chan // LANES
    per_tile = LANES * groups // chan
    n_pieces = kb // PIECE
    n_hops = max(n_ch // 2 - 1, 1)
    reduce_here = tiles == n_ctx
    dma = pltpu.SemaphoreType.DMA
    vmem = pl.BlockSpec(memory_space=pltpu.VMEM)
    hbm = pl.BlockSpec(memory_space=pl.ANY)
    n_slots = n_ctx if reduce_here else 1
    act = jax.ShapeDtypeStruct((tok, chan), BF16)
    outs = pl.pallas_call(
        functools.partial(kernel_body, n_ctx, n_ch, reduce_here),
        out_shape=(
            act, act, act, act,
            jax.ShapeDtypeStruct((tiles, per_tile, LANES), F32),
            jax.ShapeDtypeStruct((tiles, 1, LANES), F32),
        ),
        in_specs=[vmem] * 5 + [hbm] * 2,
        out_specs=(vmem,) * 6,
        scratch_shapes=[
            pltpu.VMEM((n_ch, tok, kb), BF16),
            pltpu.VMEM((n_ch, chan, kb), BF16),
            pltpu.VMEM((groups * tok, 2 * taps), BF16),
            pltpu.VMEM((groups * tok, 2 * taps), BF16),
            pltpu.VMEM((2, groups, taps), F32),
            pltpu.VMEM((2 * tok, chan), BF16),
            pltpu.VMEM((2 * tok, chan), BF16),
            pltpu.VMEM((chan, tok), F32),
            pltpu.VMEM((tok, chan), F32),
            pltpu.VMEM((2 * tok, chan), BF16),
            pltpu.VMEM((tok, chan), F32),
            pltpu.VMEM((tiles, 2 * per_tile, LANES), F32),
            pltpu.VMEM((n_slots, 2 * per_tile, LANES), F32),
            pltpu.VMEM((2 * per_tile, LANES), F32),
            pltpu.VMEM((n_slots, 2 * per_tile, LANES), F32),
            dma((n_ch,)), dma,
            dma((n_hops, n_pieces)), dma((n_hops, n_pieces)),
            dma, dma,
            dma((n_hops, n_pieces)), dma((n_hops, n_pieces)),
            dma, dma,
            dma((tiles,)), dma((tiles,)),
            dma((n_slots,)), dma((n_slots,)), dma((n_slots,)), dma((n_slots,)),
        ],
        compiler_params=pltpu.CompilerParams(
            collective_id=0, has_side_effects=True, vmem_limit_bytes=56 * 2**20),
        name="hyena",
    )(query_act, key_act, value_act, filters, skip_bias.reshape(1, chan), out_weight, out_grad)
    outs = pl.pallas_call(
        hand_on,
        out_shape=tuple(jax.ShapeDtypeStruct(x.shape, x.dtype) for x in outs),
        in_specs=[vmem] * len(outs),
        out_specs=(hbm,) * len(outs),
        scratch_shapes=[dma((len(outs),))],
        name="hand_on",
    )(*outs)
    gated, query_grad, key_grad, value_grad, filter_grad, skip_grad = outs
    filter_grad = filter_grad.reshape(groups, taps)
    skip_grad = skip_grad.reshape(chan)
    if not reduce_here:
        filter_grad, skip_grad = lax.psum((filter_grad, skip_grad), "ctx")
    return gated, query_grad, key_grad, value_grad, filter_grad, skip_grad


def solution(mesh):
    act = P("ctx", "ch")
    in_specs = (act, act, act, P("ch", None), P("ch"), P("ch", None), act)
    out_specs = (act, act, act, act, P("ch", None), P("ch"))
    return jax.shard_map(
        functools.partial(per_device, mesh.shape["ctx"], mesh.shape["ch"]),
        mesh=mesh, in_specs=in_specs, out_specs=out_specs, check_vma=False,
    )
```
